32 devices in a mesh: gx: 8 (over z, y), gy: 4 (over x, core).
Axes of the slice: x: 2, y: 2, z: 4, core: 2. Of those that a mesh axis runs over, the one named last changes fastest.
Arguments:
- spins: bfloat16 [16, 32, 256, 256], P(None, 'gx', 'gy'), may hold values from -1 to 1
- couplings: int32 [6, 32, 256, 256], P(None, 'gx', 'gy'), may hold values from -1 to 1, as said below
- betas: float32 [16], replicated, may hold values from 0.25 to 1.5
- metro_uniform: bfloat16 [2, 16, 32, 256, 256], P(None, None, 'gx', 'gy'), may hold values from 0 to 1
- swap_uniform: float32 [8], replicated, may hold values from 0.8 to 1
Outputs:
- spins_out: bfloat16 [16, 32, 256, 256], P(None, 'gx', 'gy')
- energies: float32 [16], replicated
The draws below stay inside these ranges and needn't reach their ends.
Inputs may be any that keep to these rules, and one draw needn't show every extreme that they name: Every entry is -1 or 1; couplings[3 + d] at a cell equals couplings[d] at the cell one step lower along lattice dimension d, with periodic wrap.
All inputs are finite; a program needn't handle non-finite values.
Results may differ from the reference program's by a relative error of at most 0.0085.
Values may be sent and summed in bfloat16 or wider, within the bound.
A program may use at most 128 MiB of HBM per device.

```python
import jax
import jax.numpy as jnp
from jax import lax

R = 16
SWEEPS = 2
CX = 4
CY = 64
NZ = 256
NX = 32
NY = 256


def common_signs(key):
    pattern = 2 * jax.random.randint(jax.random.fold_in(key, 5), (NX, NY, NZ), 0, 2) - 1
    return pattern


def replica_flips(key):
    return 2 * jax.random.randint(jax.random.fold_in(key, 7), (R,), 0, 2) - 1


def draw_spins(key, part):
    shape = (R, NX, NY, NZ)
    pair_count = R // 2
    x_blocks = NX // CX
    y_blocks = NY // CY
    pattern = common_signs(key)
    flips = replica_flips(key)
    aligned = (flips[:, None, None, None] * pattern[None]).astype(jnp.float32)
    scattered = (2 * jax.random.randint(jax.random.fold_in(key, 8), shape, 0, 2) - 1).astype(jnp.float32)
    position = jnp.arange(NX, dtype=jnp.float32) / jnp.float32(NX - 1)
    ramp_line = 0.55 + 0.45 * position
    x_gain = jax.random.uniform(jax.random.fold_in(key, 12), (pair_count, x_blocks), jnp.float32, 0.35, 1.0)
    y_gain = jax.random.uniform(jax.random.fold_in(key, 13), (pair_count, y_blocks), jnp.float32, 0.7, 1.0)
    spread = jax.random.uniform(jax.random.fold_in(key, 6), shape, jnp.float32, 0.7, 1.0)
    order_frac = jax.random.uniform(jax.random.fold_in(key, 14), (pair_count, x_blocks), jnp.float32, 0.0, 1.0)
    x_cells = jnp.repeat(x_gain, CX, axis=1)
    y_cells = jnp.repeat(y_gain, CY, axis=1)
    order_cells = jnp.repeat(order_frac, CX, axis=1)
    leading = ramp_line[None, :, None] * x_cells[:, :, None] * y_cells[:, None, :]
    mirrored = leading[:, ::-1, ::-1]
    amplitude = jnp.stack([leading, mirrored], axis=1).reshape(R, NX, NY)
    lead_order = jnp.broadcast_to(order_cells[:, :, None], (pair_count, NX, NY))
    order_field = jnp.stack([lead_order, lead_order[:, ::-1, ::-1]], axis=1).reshape(R, NX, NY)
    choose = jax.random.uniform(jax.random.fold_in(key, 15), shape, jnp.float32, 0.0, 1.0) < order_field[..., None]
    sign_field = jnp.where(choose, aligned, scattered)
    return (sign_field * amplitude[..., None] * spread).astype(jnp.bfloat16)


def draw_couplings(key, part):
    shape = (2, NX, NY, NZ)
    pattern = common_signs(key)
    along_x = pattern * jnp.roll(pattern, -1, 0)
    others = 2 * jax.random.randint(jax.random.fold_in(key, 11), shape, 0, 2) - 1
    forward = jnp.concatenate([along_x[None], others], axis=0)
    backward = jnp.stack([jnp.roll(forward[0], 1, 0), jnp.roll(forward[1], 1, 1), jnp.roll(forward[2], 1, 2)])
    return jnp.concatenate([forward, backward], axis=0).astype(jnp.int32)


def draw_betas(key, part):
    rungs = jnp.arange(R, dtype=jnp.float32)
    jitter = jax.random.uniform(jax.random.fold_in(key, 31), (R,), jnp.float32, -0.3, 0.3)
    levels = (rungs + 0.5 + jitter) / jnp.float32(R)
    values = 0.25 * jnp.exp(levels * jnp.log(jnp.float32(6.0)))
    return values.astype(jnp.float32)


def block_levels(stream_key, dims, split, smallest, top_value):
    gain = 1.0
    for axis_at, parts in split:
        draws = jax.random.uniform(jax.random.fold_in(jax.random.fold_in(stream_key, 6), axis_at), (parts,), jnp.float32, smallest / len(split), top_value / len(split))
        gain = gain * jnp.repeat(jnp.exp(draws), dims[axis_at] // parts).reshape((-1,) + (1,) * (len(dims) - 1 - axis_at))
    return gain


def setup_inputs(seed: int = 0) -> dict:
    seeds = jax.random.split(jax.random.key(seed), 6)
    return {
        "spins": draw_spins(jax.random.fold_in(seeds[5], 71), 0),
        "couplings": draw_couplings(jax.random.fold_in(seeds[5], 71), 0),
        "betas": draw_betas(jax.random.fold_in(seeds[5], 71), 0),
        "metro_uniform": jnp.clip(1.0 * jax.random.uniform(seeds[3], (SWEEPS, R, NX, NY, NZ), jnp.float32) ** block_levels(seeds[3], (SWEEPS, R, NX, NY, NZ), ((2, 8), (3, 4)), -0.2, 0.2), 0.0, 1.0).astype(jnp.bfloat16),
        "swap_uniform": jnp.clip(jax.random.uniform(seeds[4], (R // 2,), jnp.float32, 0.8, 1.0), 0.8, 1.0),
    }


soft_width = 0.1
swap_width = 0.25
swap_gain = 64.0


def neighbour_field(bonds, state):
    field = bonds[0] * jnp.roll(state, -1, 0) + bonds[3] * jnp.roll(state, 1, 0)
    field = field + bonds[1] * jnp.roll(state, -1, 1) + bonds[4] * jnp.roll(state, 1, 1)
    field = field + bonds[2] * jnp.roll(state, -1, 2) + bonds[5] * jnp.roll(state, 1, 2)
    return field


def reference(spins, couplings, betas, metro_uniform, swap_uniform):
    bonds = couplings.astype(jnp.float32)
    shape = (NX, NY, NZ)
    parity = (lax.broadcasted_iota(jnp.int32, shape, 0) + lax.broadcasted_iota(jnp.int32, shape, 1)
              + lax.broadcasted_iota(jnp.int32, shape, 2)) % 2

    def one_replica(index):
        state = spins[index]
        inverse = betas[index].astype(jnp.float32)
        for sweep in range(SWEEPS):
            uniform = metro_uniform[sweep, index].astype(jnp.float32)
            for colour in (0, 1):
                current = state.astype(jnp.float32)
                field = neighbour_field(bonds, current)
                accept = jnp.exp(-inverse * jnp.maximum(2.0 * current * field, 0.0))
                weight = jax.nn.sigmoid((accept - uniform) / soft_width)
                flipped = current * (1.0 - 2.0 * weight)
                state = jnp.where(parity == colour, flipped, current).astype(jnp.bfloat16)
        current = state.astype(jnp.float32)
        bond_sum = bonds[0] * current * jnp.roll(current, -1, 0)
        bond_sum = bond_sum + bonds[1] * current * jnp.roll(current, -1, 1)
        bond_sum = bond_sum + bonds[2] * current * jnp.roll(current, -1, 2)
        energy = -jnp.sum(bond_sum) / jnp.float32(NX * NY * NZ)
        return state, energy

    swept, energies = lax.map(one_replica, jnp.arange(R, dtype=jnp.int32))
    first_e = energies[0::2]
    second_e = energies[1::2]
    delta = swap_gain * (betas[0::2] - betas[1::2]) * (first_e - second_e)
    mix = jax.nn.sigmoid((jnp.minimum(delta, 0.0) - jnp.log(swap_uniform)) / swap_width)
    paired = swept.reshape(R // 2, 2, NX, NY, NZ)

    def one_pair(item):
        pair, weight = item
        upper = pair[0].astype(jnp.float32)
        lower = pair[1].astype(jnp.float32)
        new_upper = (1.0 - weight) * upper + weight * lower
        new_lower = (1.0 - weight) * lower + weight * upper
        return jnp.stack([new_upper, new_lower]).astype(jnp.bfloat16)

    mixed = lax.map(one_pair, (paired, mix))
    return mixed.reshape(R, NX, NY, NZ), energies
```

```python
import functools

import jax
import jax.numpy as jnp
from jax import lax
from jax.experimental import pallas as pl
from jax.experimental.pallas import tpu as pltpu
from jax.sharding import PartitionSpec as P

MESH = pl.DeviceIdType.MESH
LOG2E = 1.4426950408889634
PAD = 8
ROWS = 16

soft_width = 0.1
swap_width = 0.25
swap_gain = 64.0


def kernel(
    nx, ny, group,
    spins, bonds, metro, betas, swaps,
    swept, energy_out, mix_out,
    state, weights, xsend, xrecv, ysend, yrecv, esum, erow, eslot_y, eslot_x,
    ssem, rsem, esend, erecv,
):
    replicas, cells_x, cells_y, cells_z = spins.shape
    sweeps = metro.shape[0]
    pairs = cells_x // 2
    half = cells_y // 2
    groups = replicas // group
    chunks = cells_y // ROWS
    steps = 2 * sweeps
    gx = lax.axis_index("gx")
    gy = lax.axis_index("gy")
    up_x, down_x = lax.rem(gx + 1, nx), lax.rem(gx + nx - 1, nx)
    up_y, down_y = lax.rem(gy + 1, ny), lax.rem(gy + ny - 1, ny)

    barrier = pltpu.get_barrier_semaphore()
    for k in range(1, nx):
        pl.semaphore_signal(barrier, inc=1, device_id=(lax.rem(gx + k, nx), gy), device_id_type=MESH)
    for k in range(1, ny):
        pl.semaphore_signal(barrier, inc=1, device_id=(gx, lax.rem(gy + k, ny)), device_id_type=MESH)

    yz = lax.broadcasted_iota(jnp.int32, (ROWS, cells_z), 0) + lax.broadcasted_iota(jnp.int32, (ROWS, cells_z), 1)
    even = (yz & 1) == 0

    def low(colour):
        return even if colour == 0 else jnp.logical_not(even)

    def copies(t, g):
        out = []
        for side, target in enumerate(((up_x, gy), (down_x, gy))):
            out.append(pltpu.make_async_remote_copy(
                src_ref=xsend.at[t, g, side], dst_ref=xrecv.at[t, g, side],
                send_sem=ssem.at[t, g, side], recv_sem=rsem.at[t, g, side],
                device_id=target, device_id_type=MESH))
        for side, target in enumerate(((gx, up_y), (gx, down_y))):
            out.append(pltpu.make_async_remote_copy(
                src_ref=ysend.at[t, g, side], dst_ref=yrecv.at[t, g, side],
                send_sem=ssem.at[t, g, 2 + side], recv_sem=rsem.at[t, g, 2 + side],
                device_id=target, device_id_type=MESH))
        return out

    def pack_faces(t, g, rr, r):
        colour = t % 2
        mask = low(colour)
        other = 1 - colour
        for y0 in range(0, half, ROWS):
            for side, plane in ((0, pairs - 1), (1, 0)):
                near = state[other, r, plane, pl.ds(PAD + y0, ROWS), :]
                far = pltpu.roll(state[other, r, plane, pl.ds(PAD + half + y0, ROWS), :], 1, 1)
                face = jnp.where(mask, near, far) if side == 0 else jnp.where(mask, far, near)
                xsend[t, g, side, rr, pl.ds(y0, ROWS), :] = face.astype(jnp.bfloat16)
        for i in range(pairs):
            ysend[t, g, 0, pl.ds(rr * pairs + i, 1), :] = state[other, r, i, pl.ds(PAD + cells_y - 1, 1), :]
            ysend[t, g, 1, pl.ds(rr * pairs + i, 1), :] = state[other, r, i, pl.ds(PAD, 1), :]

    def first_group(g, carry):
        def one(rr, c):
            r = g * group + rr
            for i in range(pairs):
                for n in range(chunks):
                    rows = pl.ds(n * ROWS, ROWS)
                    a = spins[r, 2 * i, rows, :].astype(jnp.float32)
                    b = spins[r, 2 * i + 1, rows, :].astype(jnp.float32)
                    state[0, r, i, pl.ds(PAD + n * ROWS, ROWS), :] = jnp.where(even, a, b)
                    state[1, r, i, pl.ds(PAD + n * ROWS, ROWS), :] = jnp.where(even, b, a)
            pack_faces(0, g, rr, r)
            return c
        lax.fori_loop(0, group, one, 0)
        for copy in copies(0, g):
            copy.start()
        return carry

    pl.semaphore_wait(barrier, nx + ny - 2)
    lax.fori_loop(0, groups, first_group, 0)

    def weigh(n, carry):
        rows = pl.ds(pl.multiple_of(n * ROWS, ROWS), ROWS)
        for colour in (0, 1):
            mask = low(colour)
            for i in range(pairs):
                lo, hi = 2 * i, 2 * i + 1
                table = ((0, 3), (3, 0), (1, 1), (4, 4), (2, 2), (5, 5))
                for k, (p, q) in enumerate(table):
                    value = jnp.where(mask, bonds[p, lo, rows, :], bonds[q, hi, rows, :])
                    weights[colour, k, i, rows, :] = value.astype(jnp.float32)
        return carry

    lax.fori_loop(0, chunks, weigh, 0)

    for t in range(steps):
        colour, sweep, other = t % 2, t // 2, 1 - t % 2
        mask = low(colour)
        last = t == steps - 1

        def one_group(g, carry, t=t, colour=colour, sweep=sweep, other=other, mask=mask, last=last):
            for copy in copies(t, g):
                copy.wait_recv()

            def one(rr, c):
                r = g * group + rr
                gain = betas[r] * (-2.0 * LOG2E)
                for i in range(pairs):
                    row = pl.ds(rr * pairs + i, 1)
                    state[other, r, i, pl.ds(PAD - 1, 1), :] = yrecv[t, g, 0, row, :]
                    state[other, r, i, pl.ds(PAD + cells_y, 1), :] = yrecv[t, g, 1, row, :]
                total = jnp.zeros((ROWS, cells_z), jnp.float32)
                for i in range(pairs):
                    for n in range(chunks):
                        y0 = n * ROWS
                        rows = pl.ds(y0, ROWS)
                        inner = pl.ds(PAD + y0, ROWS)
                        w = [weights[colour, k, i, rows, :] for k in range(6)]

                        def halo(side):
                            face = xrecv[t, g, side, rr, pl.ds(y0 % half, ROWS), :].astype(jnp.float32)
                            return face if y0 < half else pltpu.roll(face, cells_z - 1, 1)

                        mid = state[other, r, i, inner, :]
                        below = state[other, r, i - 1, inner, :] if i > 0 else halo(0)
                        above = state[other, r, i + 1, inner, :] if i < pairs - 1 else halo(1)
                        field = w[0] * mid + w[1] * jnp.where(mask, below, above)
                        field = field + w[2] * state[other, r, i, pl.ds(PAD + y0 + 1, ROWS), :]
                        field = field + w[3] * state[other, r, i, pl.ds(PAD + y0 - 1, ROWS), :]
                        field = field + w[4] * pltpu.roll(mid, cells_z - 1, 1) + w[5] * pltpu.roll(mid, 1, 1)
                        s = state[colour, r, i, inner, :]
                        u_lo = metro[sweep, r, 2 * i, rows, :].astype(jnp.float32)
                        u_hi = metro[sweep, r, 2 * i + 1, rows, :].astype(jnp.float32)
                        u = jnp.where(mask, u_lo, u_hi)
                        accept = jnp.exp2(jnp.minimum(s * field * gain, 0.0))
                        new = s * jnp.tanh((u - accept) * (0.5 / soft_width))
                        rounded = new.astype(jnp.bfloat16)
                        s = rounded.astype(jnp.float32)
                        if last:
                            total = total + s * field
                            a = jnp.where(even, mid, s)
                            b = jnp.where(even, s, mid)
                            swept[r, 2 * i, rows, :] = a.astype(jnp.bfloat16)
                            swept[r, 2 * i + 1, rows, :] = b.astype(jnp.bfloat16)
                        else:
                            state[colour, r, i, inner, :] = s
                if last:
                    esum[lax.rem(r, 2), pl.ds(r // 2, 1), :] = jnp.sum(total, axis=0, keepdims=True)
                else:
                    pack_faces(t + 1, g, rr, r)
                return c

            lax.fori_loop(0, group, one, 0)
            if not last:
                for copy in copies(t + 1, g):
                    copy.start()
            return carry

        lax.fori_loop(0, groups, one_group, 0)

    def share(value, slots, n, mine, sem0, device):
        erow[sem0] = value
        slots[mine] = value
        sends = []
        for k in range(1, n):
            copy = pltpu.make_async_remote_copy(
                src_ref=erow.at[sem0], dst_ref=slots.at[mine],
                send_sem=esend.at[sem0, k], recv_sem=erecv.at[sem0, k],
                device_id=device(lax.rem(mine + k, n)), device_id_type=MESH)
            copy.start()
            sends.append(copy)
        for copy in sends:
            copy.wait()
        total = slots[0]
        for k in range(1, n):
            total = total + slots[k]
        return total

    mine = jnp.sum(esum[...], axis=2, keepdims=True) + jnp.zeros(erow.shape[1:], jnp.float32)
    total = share(mine, eslot_y, ny, gy, 0, lambda d: (gx, d))
    total = share(total, eslot_x, nx, gx, 1, lambda d: (d, gy))
    energies = total * (-1.0 / (cells_x * nx * cells_y * ny * cells_z))
    energy_out[...] = energies
    row = lax.broadcasted_iota(jnp.int32, erow.shape[2:], 0)
    gap = jnp.zeros(erow.shape[2:], jnp.float32)
    draw = jnp.ones(erow.shape[2:], jnp.float32)
    for k in range(replicas // 2):
        gap = jnp.where(row == k, betas[2 * k] - betas[2 * k + 1], gap)
        draw = jnp.where(row == k, swaps[k], draw)
    delta = swap_gain * gap * (energies[0] - energies[1])
    mix_out[...] = jax.nn.sigmoid((jnp.minimum(delta, 0.0) - jnp.log(draw)) / swap_width)

    def finish(g, carry):
        for t in range(steps):
            for copy in copies(t, g):
                copy.wait_send()
        return carry

    lax.fori_loop(0, groups, finish, 0)


def solution(mesh):
    nx, ny = mesh.shape["gx"], mesh.shape["gy"]

    def body(spins, couplings, betas, metro_uniform, swap_uniform):
        replicas, cells_x, cells_y, cells_z = spins.shape
        sweeps = metro_uniform.shape[0]
        pairs, steps, duos = cells_x // 2, 2 * sweeps, replicas // 2
        group = 8 // pairs
        groups = replicas // group
        f32, bf16 = jnp.float32, jnp.bfloat16
        vmem = pl.BlockSpec(memory_space=pltpu.VMEM)
        smem = pl.BlockSpec(memory_space=pltpu.SMEM)
        lanes = 128
        xface = (steps, groups, 2, group, cells_y // 2, cells_z)
        yface = (steps, groups, 2, group * pairs, cells_z)
        swept, energy, mix = pl.pallas_call(
            functools.partial(kernel, nx, ny, group),
            out_shape=(
                jax.ShapeDtypeStruct(spins.shape, bf16),
                jax.ShapeDtypeStruct((2, duos, lanes), f32),
                jax.ShapeDtypeStruct((duos, lanes), f32),
            ),
            in_specs=[vmem, vmem, vmem, smem, smem],
            out_specs=(vmem, vmem, vmem),
            scratch_shapes=[
                pltpu.VMEM((2, replicas, pairs, cells_y + 2 * PAD, cells_z), f32),
                pltpu.VMEM((2, 6, pairs, cells_y, cells_z), f32),
                pltpu.VMEM(xface, bf16),
                pltpu.VMEM(xface, bf16),
                pltpu.VMEM(yface, f32),
                pltpu.VMEM(yface, f32),
                pltpu.VMEM((2, duos, cells_z), f32),
                pltpu.VMEM((2, 2, duos, lanes), f32),
                pltpu.VMEM((ny, 2, duos, lanes), f32),
                pltpu.VMEM((nx, 2, duos, lanes), f32),
                pltpu.SemaphoreType.DMA((steps, groups, 4)),
                pltpu.SemaphoreType.DMA((steps, groups, 4)),
                pltpu.SemaphoreType.DMA((2, max(nx, ny))),
                pltpu.SemaphoreType.DMA((2, max(nx, ny))),
            ],
            compiler_params=pltpu.CompilerParams(
                collective_id=0, has_side_effects=True, vmem_limit_bytes=48 * 1024 * 1024
            ),
        )(spins, couplings, metro_uniform, betas, swap_uniform)
        paired = swept.reshape(duos, 2, cells_x, cells_y, cells_z).astype(f32)
        weight = mix[:, 0][:, None, None, None, None]
        mixed = ((1.0 - weight) * paired + weight * paired[:, ::-1]).astype(bf16)
        return mixed.reshape(spins.shape), energy[:, :, 0].T.reshape(replicas)

    in_specs = (
        P(None, "gx", "gy", None),
        P(None, "gx", "gy", None),
        P(),
        P(None, None, "gx", "gy", None),
        P(),
    )
    out_specs = (P(None, "gx", "gy", None), P())
    return jax.shard_map(body, mesh=mesh, in_specs=in_specs, out_specs=out_specs, check_vma=False)
```

```python
import functools

import jax
import jax.numpy as jnp
from jax import lax
from jax.experimental import pallas as pl
from jax.experimental.pallas import tpu as pltpu
from jax.sharding import PartitionSpec as P

MESH = pl.DeviceIdType.MESH
LOG2E = 1.4426950408889634
PAD = 8
ROWS = 16

soft_width = 0.1
swap_width = 0.25
swap_gain = 64.0


def kernel(
    nx, ny, group,
    spins_hbm, bonds_hbm, metro_hbm, betas, swaps,
    swept_hbm, info_out,
    spins, bonds, metro, swept, spins_sem, bonds_sem, metro_sem, swept_sem,
    state, weights, xsend, xrecv, ysend, yrecv, esum, erow, eslot_y, eslot_x,
    ssem, rsem, esend, erecv,
):
    replicas, cells_x, cells_y, cells_z = spins.shape
    sweeps = metro.shape[0]
    pairs = cells_x // 2
    half = cells_y // 2
    groups = replicas // group
    chunks = cells_y // ROWS
    steps = 2 * sweeps
    gx = lax.axis_index("gx")
    gy = lax.axis_index("gy")
    up_x, down_x = lax.rem(gx + 1, nx), lax.rem(gx + nx - 1, nx)
    up_y, down_y = lax.rem(gy + 1, ny), lax.rem(gy + ny - 1, ny)

    def part(g):
        return pl.ds(g * group, group)

    def spins_in(g):
        return pltpu.make_async_copy(spins_hbm.at[part(g)], spins.at[part(g)], spins_sem.at[g])

    def metro_in(sweep, g):
        return pltpu.make_async_copy(
            metro_hbm.at[sweep, part(g)], metro.at[sweep, part(g)], metro_sem.at[sweep, g])

    def swept_to(g):
        return pltpu.make_async_copy(swept.at[part(g)], swept_hbm.at[part(g)], swept_sem.at[g])

    bonds_in = pltpu.make_async_copy(bonds_hbm, bonds, bonds_sem)
    for g in range(groups):
        spins_in(g).start()

    barrier = pltpu.get_barrier_semaphore()
    for k in range(1, nx):
        pl.semaphore_signal(barrier, inc=1, device_id=(lax.rem(gx + k, nx), gy), device_id_type=MESH)
    for k in range(1, ny):
        pl.semaphore_signal(barrier, inc=1, device_id=(gx, lax.rem(gy + k, ny)), device_id_type=MESH)

    bonds_in.start()
    for sweep in range(sweeps):
        for g in range(groups):
            metro_in(sweep, g).start()

    yz = lax.broadcasted_iota(jnp.int32, (ROWS, cells_z), 0) + lax.broadcasted_iota(jnp.int32, (ROWS, cells_z), 1)
    even = (yz & 1) == 0

    def low(colour):
        return even if colour == 0 else jnp.logical_not(even)

    def copies(t, g):
        out = []
        for side, target in enumerate(((up_x, gy), (down_x, gy))):
            out.append(pltpu.make_async_remote_copy(
                src_ref=xsend.at[t, g, side], dst_ref=xrecv.at[t, g, side],
                send_sem=ssem.at[t, g, side], recv_sem=rsem.at[t, g, side],
                device_id=target, device_id_type=MESH))
        for side, target in enumerate(((gx, up_y), (gx, down_y))):
            out.append(pltpu.make_async_remote_copy(
                src_ref=ysend.at[t, g, side], dst_ref=yrecv.at[t, g, side],
                send_sem=ssem.at[t, g, 2 + side], recv_sem=rsem.at[t, g, 2 + side],
                device_id=target, device_id_type=MESH))
        return out

    def pack_faces(t, g, rr, r):
        colour = t % 2
        mask = low(colour)
        other = 1 - colour
        for y0 in range(0, half, ROWS):
            for side, plane in ((0, pairs - 1), (1, 0)):
                near = state[other, r, plane, pl.ds(PAD + y0, ROWS), :]
                far = pltpu.roll(state[other, r, plane, pl.ds(PAD + half + y0, ROWS), :], 1, 1)
                face = jnp.where(mask, near, far) if side == 0 else jnp.where(mask, far, near)
                xsend[t, g, side, rr, pl.ds(y0, ROWS), :] = face.astype(jnp.bfloat16)
        for i in range(pairs):
            ysend[t, g, 0, pl.ds(rr * pairs + i, 1), :] = state[other, r, i, pl.ds(PAD + cells_y - 1, 1), :]
            ysend[t, g, 1, pl.ds(rr * pairs + i, 1), :] = state[other, r, i, pl.ds(PAD, 1), :]

    def prepare(g):
        spins_in(g).wait()

        def one(rr, c):
            r = g * group + rr
            for i in range(pairs):
                for n in range(chunks):
                    rows = pl.ds(n * ROWS, ROWS)
                    a = spins[r, 2 * i, rows, :].astype(jnp.float32)
                    b = spins[r, 2 * i + 1, rows, :].astype(jnp.float32)
                    state[0, r, i, pl.ds(PAD + n * ROWS, ROWS), :] = jnp.where(even, a, b)
                    state[1, r, i, pl.ds(PAD + n * ROWS, ROWS), :] = jnp.where(even, b, a)
            pack_faces(0, g, rr, r)
            return c
        lax.fori_loop(0, group, one, 0)

    def first_group(g, carry):
        prepare(g)
        for copy in copies(0, g):
            copy.start()
        return carry

    prepare(0)
    pl.semaphore_wait(barrier, nx + ny - 2)
    for copy in copies(0, 0):
        copy.start()
    lax.fori_loop(1, groups, first_group, 0)
    bonds_in.wait()

    def weigh(n, carry):
        rows = pl.ds(pl.multiple_of(n * ROWS, ROWS), ROWS)
        for colour in (0, 1):
            mask = low(colour)
            for i in range(pairs):
                lo, hi = 2 * i, 2 * i + 1
                table = ((0, 3), (3, 0), (1, 1), (4, 4), (2, 2), (5, 5))
                for k, (p, q) in enumerate(table):
                    value = jnp.where(mask, bonds[p, lo, rows, :], bonds[q, hi, rows, :])
                    weights[colour, k, i, rows, :] = value.astype(jnp.float32)
        return carry

    lax.fori_loop(0, chunks, weigh, 0)

    for t in range(steps):
        colour, sweep, other = t % 2, t // 2, 1 - t % 2
        mask = low(colour)
        last = t == steps - 1

        def one_group(g, carry, t=t, colour=colour, sweep=sweep, other=other, mask=mask, last=last):
            if colour == 0:
                metro_in(sweep, g).wait()
            for copy in copies(t, g):
                copy.wait_recv()

            def one(rr, c):
                r = g * group + rr
                gain = betas[r] * (-2.0 * LOG2E)
                for i in range(pairs):
                    row = pl.ds(rr * pairs + i, 1)
                    state[other, r, i, pl.ds(PAD - 1, 1), :] = yrecv[t, g, 0, row, :]
                    state[other, r, i, pl.ds(PAD + cells_y, 1), :] = yrecv[t, g, 1, row, :]
                total = jnp.zeros((ROWS, cells_z), jnp.float32)
                for i in range(pairs):
                    for n in range(chunks):
                        y0 = n * ROWS
                        rows = pl.ds(y0, ROWS)
                        inner = pl.ds(PAD + y0, ROWS)
                        w = [weights[colour, k, i, rows, :] for k in range(6)]

                        def halo(side):
                            face = xrecv[t, g, side, rr, pl.ds(y0 % half, ROWS), :].astype(jnp.float32)
                            return face if y0 < half else pltpu.roll(face, cells_z - 1, 1)

                        mid = state[other, r, i, inner, :]
                        below = state[other, r, i - 1, inner, :] if i > 0 else halo(0)
                        above = state[other, r, i + 1, inner, :] if i < pairs - 1 else halo(1)
                        field = w[0] * mid + w[1] * jnp.where(mask, below, above)
                        field = field + w[2] * state[other, r, i, pl.ds(PAD + y0 + 1, ROWS), :]
                        field = field + w[3] * state[other, r, i, pl.ds(PAD + y0 - 1, ROWS), :]
                        field = field + w[4] * pltpu.roll(mid, cells_z - 1, 1) + w[5] * pltpu.roll(mid, 1, 1)
                        s = state[colour, r, i, inner, :]
                        u_lo = metro[sweep, r, 2 * i, rows, :].astype(jnp.float32)
                        u_hi = metro[sweep, r, 2 * i + 1, rows, :].astype(jnp.float32)
                        u = jnp.where(mask, u_lo, u_hi)
                        accept = jnp.exp2(jnp.minimum(s * field * gain, 0.0))
                        new = s * jnp.tanh((u - accept) * (0.5 / soft_width))
                        rounded = new.astype(jnp.bfloat16)
                        s = rounded.astype(jnp.float32)
                        if last:
                            total = total + s * field
                            a = jnp.where(even, mid, s)
                            b = jnp.where(even, s, mid)
                            swept[r, 2 * i, rows, :] = a.astype(jnp.bfloat16)
                            swept[r, 2 * i + 1, rows, :] = b.astype(jnp.bfloat16)
                        else:
                            state[colour, r, i, inner, :] = s
                if last:
                    esum[lax.rem(r, 2), pl.ds(r // 2, 1), :] = jnp.sum(total, axis=0, keepdims=True)
                else:
                    pack_faces(t + 1, g, rr, r)
                return c

            lax.fori_loop(0, group, one, 0)
            if last:
                swept_to(g).start()
            else:
                for copy in copies(t + 1, g):
                    copy.start()
            for copy in copies(t, g):
                copy.wait_send()
            return carry

        lax.fori_loop(0, groups, one_group, 0)

    def share(value, slots, n, mine, sem0, device):
        erow[sem0] = value
        slots[mine] = value
        sends = []
        for k in range(1, n):
            copy = pltpu.make_async_remote_copy(
                src_ref=erow.at[sem0], dst_ref=slots.at[mine],
                send_sem=esend.at[sem0, k], recv_sem=erecv.at[sem0, k],
                device_id=device(lax.rem(mine + k, n)), device_id_type=MESH)
            copy.start()
            sends.append(copy)
        for copy in sends:
            copy.wait()
        total = slots[0]
        for k in range(1, n):
            total = total + slots[k]
        return total

    mine = jnp.sum(esum[...], axis=2, keepdims=True) + jnp.zeros(erow.shape[1:], jnp.float32)
    total = share(mine, eslot_y, ny, gy, 0, lambda d: (gx, d))
    total = share(total, eslot_x, nx, gx, 1, lambda d: (d, gy))
    energies = total * (-1.0 / (cells_x * nx * cells_y * ny * cells_z))
    row = lax.broadcasted_iota(jnp.int32, erow.shape[2:], 0)
    gap = jnp.zeros(erow.shape[2:], jnp.float32)
    draw = jnp.ones(erow.shape[2:], jnp.float32)
    for k in range(replicas // 2):
        gap = jnp.where(row == k, betas[2 * k] - betas[2 * k + 1], gap)
        draw = jnp.where(row == k, swaps[k], draw)
    delta = swap_gain * gap * (energies[0] - energies[1])
    mix = jax.nn.sigmoid((jnp.minimum(delta, 0.0) - jnp.log(draw)) / swap_width)
    lane = lax.broadcasted_iota(jnp.int32, erow.shape[2:], 1)
    spread = jnp.where(lane == 2 * row, energies[0], 0.0) + jnp.where(lane == 2 * row + 1, energies[1], 0.0)
    info_out[0:1, :] = jnp.sum(spread, axis=0, keepdims=True)
    info_out[1:2, :] = jnp.sum(jnp.where(lane == row, mix, 0.0), axis=0, keepdims=True)
    for g in range(groups):
        swept_to(g).wait()


def exchange(per, info, swept, out, energy_out):
    step = pl.program_id(0)

    @pl.when(step == 0)
    def _():
        for r in range(energy_out.shape[0]):
            energy_out[r] = info[0, r]

    for k in range(per):
        weight = info[1, step * per + k]
        upper = swept[2 * k].astype(jnp.float32)
        lower = swept[2 * k + 1].astype(jnp.float32)
        out[2 * k] = ((1.0 - weight) * upper + weight * lower).astype(jnp.bfloat16)
        out[2 * k + 1] = ((1.0 - weight) * lower + weight * upper).astype(jnp.bfloat16)


def solution(mesh):
    nx, ny = mesh.shape["gx"], mesh.shape["gy"]

    def body(spins, couplings, betas, metro_uniform, swap_uniform):
        replicas, cells_x, cells_y, cells_z = spins.shape
        sweeps = metro_uniform.shape[0]
        pairs, steps, duos = cells_x // 2, 2 * sweeps, replicas // 2
        group = 8 // pairs
        groups = replicas // group
        f32, bf16 = jnp.float32, jnp.bfloat16
        vmem = pl.BlockSpec(memory_space=pltpu.VMEM)
        hbm = pl.BlockSpec(memory_space=pl.ANY)
        smem = pl.BlockSpec(memory_space=pltpu.SMEM)
        lanes = 128
        xface = (steps, groups, 2, group, cells_y // 2, cells_z)
        yface = (steps, groups, 2, group * pairs, cells_z)
        swept, info = pl.pallas_call(
            functools.partial(kernel, nx, ny, group),
            out_shape=(
                jax.ShapeDtypeStruct(spins.shape, bf16),
                jax.ShapeDtypeStruct((2, lanes), f32),
            ),
            in_specs=[hbm, hbm, hbm, smem, smem],
            out_specs=(hbm, vmem),
            scratch_shapes=[
                pltpu.VMEM(spins.shape, bf16),
                pltpu.VMEM(couplings.shape, jnp.int32),
                pltpu.VMEM(metro_uniform.shape, bf16),
                pltpu.VMEM(spins.shape, bf16),
                pltpu.SemaphoreType.DMA((groups,)),
                pltpu.SemaphoreType.DMA,
                pltpu.SemaphoreType.DMA((sweeps, groups)),
                pltpu.SemaphoreType.DMA((groups,)),
                pltpu.VMEM((2, replicas, pairs, cells_y + 2 * PAD, cells_z), f32),
                pltpu.VMEM((2, 6, pairs, cells_y, cells_z), f32),
                pltpu.VMEM(xface, bf16),
                pltpu.VMEM(xface, bf16),
                pltpu.VMEM(yface, f32),
                pltpu.VMEM(yface, f32),
                pltpu.VMEM((2, duos, cells_z), f32),
                pltpu.VMEM((2, 2, duos, lanes), f32),
                pltpu.VMEM((ny, 2, duos, lanes), f32),
                pltpu.VMEM((nx, 2, duos, lanes), f32),
                pltpu.SemaphoreType.DMA((steps, groups, 4)),
                pltpu.SemaphoreType.DMA((steps, groups, 4)),
                pltpu.SemaphoreType.DMA((2, max(nx, ny))),
                pltpu.SemaphoreType.DMA((2, max(nx, ny))),
            ],
            compiler_params=pltpu.CompilerParams(
                collective_id=0, has_side_effects=True, vmem_limit_bytes=60 * 1024 * 1024
            ),
        )(spins, couplings, metro_uniform, betas, swap_uniform)
        per = 2
        block = pl.BlockSpec((2 * per,) + spins.shape[1:], lambda k: (k, 0, 0, 0))
        return pl.pallas_call(
            functools.partial(exchange, per),
            grid=(duos // per,),
            out_shape=(
                jax.ShapeDtypeStruct(spins.shape, bf16),
                jax.ShapeDtypeStruct((replicas,), f32),
            ),
            in_specs=[smem, block],
            out_specs=(block, smem),
        )(info, swept)

    in_specs = (
        P(None, "gx", "gy", None),
        P(None, "gx", "gy", None),
        P(),
        P(None, None, "gx", "gy", None),
        P(),
    )
    out_specs = (P(None, "gx", "gy", None), P())
    return jax.shard_map(body, mesh=mesh, in_specs=in_specs, out_specs=out_specs, check_vma=False)
```

```python
import functools

import jax
import jax.numpy as jnp
from jax import lax
from jax.experimental import pallas as pl
from jax.experimental.pallas import tpu as pltpu
from jax.sharding import PartitionSpec as P

MESH = pl.DeviceIdType.MESH
LOG2E = 1.4426950408889634
PAD = 8
ROWS = 16

soft_width = 0.1
swap_width = 0.25
swap_gain = 64.0


def kernel(
    nx, ny, group,
    spins_hbm, bonds_hbm, metro_hbm, betas, swaps,
    swept_hbm, info_out,
    spins, bonds, metro, swept, spins_sem, bonds_sem, metro_sem, swept_sem,
    state, weights, xsend, xrecv, ysend, yrecv, esum, erow, eslot_y, eslot_x,
    ssem, rsem, esend, erecv,
):
    replicas, cells_x, cells_y, cells_z = spins.shape
    sweeps = metro.shape[0]
    pairs = cells_x // 2
    half = cells_y // 2
    groups = replicas // group
    chunks = cells_y // ROWS
    steps = 2 * sweeps
    gx = lax.axis_index("gx")
    gy = lax.axis_index("gy")
    up_x, down_x = lax.rem(gx + 1, nx), lax.rem(gx + nx - 1, nx)
    up_y, down_y = lax.rem(gy + 1, ny), lax.rem(gy + ny - 1, ny)

    def part(g):
        return pl.ds(g * group, group)

    def spins_in(g):
        return pltpu.make_async_copy(spins_hbm.at[part(g)], spins.at[part(g)], spins_sem.at[g])

    def metro_in(sweep, g):
        return pltpu.make_async_copy(
            metro_hbm.at[sweep, part(g)], metro.at[sweep, part(g)], metro_sem.at[sweep, g])

    def swept_to(g):
        return pltpu.make_async_copy(swept.at[part(g)], swept_hbm.at[part(g)], swept_sem.at[g])

    bonds_in = pltpu.make_async_copy(bonds_hbm, bonds, bonds_sem)
    for g in range(groups):
        spins_in(g).start()

    barrier = pltpu.get_barrier_semaphore()
    for k in range(1, nx):
        pl.semaphore_signal(barrier, inc=1, device_id=(lax.rem(gx + k, nx), gy), device_id_type=MESH)
    for k in range(1, ny):
        pl.semaphore_signal(barrier, inc=1, device_id=(gx, lax.rem(gy + k, ny)), device_id_type=MESH)

    bonds_in.start()
    for sweep in range(sweeps):
        for g in range(groups):
            metro_in(sweep, g).start()

    yz = lax.broadcasted_iota(jnp.int32, (ROWS, cells_z), 0) + lax.broadcasted_iota(jnp.int32, (ROWS, cells_z), 1)
    even = (yz & 1) == 0

    def low(colour):
        return even if colour == 0 else jnp.logical_not(even)

    def copies(t, g):
        out = []
        for side, target in enumerate(((up_x, gy), (down_x, gy))):
            out.append(pltpu.make_async_remote_copy(
                src_ref=xsend.at[t, g, side], dst_ref=xrecv.at[t, g, side],
                send_sem=ssem.at[t, g, side], recv_sem=rsem.at[t, g, side],
                device_id=target, device_id_type=MESH))
        for side, target in enumerate(((gx, up_y), (gx, down_y))):
            out.append(pltpu.make_async_remote_copy(
                src_ref=ysend.at[t, g, side], dst_ref=yrecv.at[t, g, side],
                send_sem=ssem.at[t, g, 2 + side], recv_sem=rsem.at[t, g, 2 + side],
                device_id=target, device_id_type=MESH))
        return out

    def pack_faces(t, g, rr, r):
        colour = t % 2
        mask = low(colour)
        other = 1 - colour
        for y0 in range(0, half, ROWS):
            for side, plane in ((0, pairs - 1), (1, 0)):
                near = state[other, r, plane, pl.ds(PAD + y0, ROWS), :]
                far = pltpu.roll(state[other, r, plane, pl.ds(PAD + half + y0, ROWS), :], 1, 1)
                face = jnp.where(mask, near, far) if side == 0 else jnp.where(mask, far, near)
                xsend[t, g, side, rr, pl.ds(y0, ROWS), :] = face.astype(jnp.bfloat16)
        for i in range(pairs):
            ysend[t, g, 0, pl.ds(rr * pairs + i, 1), :] = state[other, r, i, pl.ds(PAD + cells_y - 1, 1), :]
            ysend[t, g, 1, pl.ds(rr * pairs + i, 1), :] = state[other, r, i, pl.ds(PAD, 1), :]

    def prepare(g):
        spins_in(g).wait()

        def one(rr, c):
            r = g * group + rr
            for i in range(pairs):
                for n in range(chunks):
                    rows = pl.ds(n * ROWS, ROWS)
                    a = spins[r, 2 * i, rows, :].astype(jnp.float32)
                    b = spins[r, 2 * i + 1, rows, :].astype(jnp.float32)
                    state[0, r, i, pl.ds(PAD + n * ROWS, ROWS), :] = jnp.where(even, a, b)
                    state[1, r, i, pl.ds(PAD + n * ROWS, ROWS), :] = jnp.where(even, b, a)
            pack_faces(0, g, rr, r)
            return c
        lax.fori_loop(0, group, one, 0)

    def first_group(g, carry):
        prepare(g)
        for copy in copies(0, g):
            copy.start()
        return carry

    prepare(0)
    pl.semaphore_wait(barrier, nx + ny - 2)
    for copy in copies(0, 0):
        copy.start()
    lax.fori_loop(1, groups, first_group, 0)
    bonds_in.wait()

    def weigh(n, carry):
        rows = pl.ds(pl.multiple_of(n * ROWS, ROWS), ROWS)
        for colour in (0, 1):
            mask = low(colour)
            for i in range(pairs):
                lo, hi = 2 * i, 2 * i + 1
                table = ((0, 3), (3, 0), (1, 1), (4, 4), (2, 2), (5, 5))
                for k, (p, q) in enumerate(table):
                    value = jnp.where(mask, bonds[p, lo, rows, :], bonds[q, hi, rows, :])
                    weights[colour, k, i, rows, :] = value.astype(jnp.float32)
        return carry

    lax.fori_loop(0, chunks, weigh, 0)

    for t in range(steps):
        colour, sweep, other = t % 2, t // 2, 1 - t % 2
        mask = low(colour)
        last = t == steps - 1

        def one_group(g, carry, t=t, colour=colour, sweep=sweep, other=other, mask=mask, last=last):
            if colour == 0:
                metro_in(sweep, g).wait()
            for copy in copies(t, g):
                copy.wait_recv()

            def one(rr, c):
                r = g * group + rr
                gain = betas[r] * (-2.0 * LOG2E)
                for i in range(pairs):
                    row = pl.ds(rr * pairs + i, 1)
                    state[other, r, i, pl.ds(PAD - 1, 1), :] = yrecv[t, g, 0, row, :]
                    state[other, r, i, pl.ds(PAD + cells_y, 1), :] = yrecv[t, g, 1, row, :]
                total = jnp.zeros((ROWS, cells_z), jnp.float32)
                for i in range(pairs):
                    for n in range(chunks):
                        y0 = n * ROWS
                        rows = pl.ds(y0, ROWS)
                        inner = pl.ds(PAD + y0, ROWS)
                        w = [weights[colour, k, i, rows, :] for k in range(6)]

                        def halo(side):
                            face = xrecv[t, g, side, rr, pl.ds(y0 % half, ROWS), :].astype(jnp.float32)
                            return face if y0 < half else pltpu.roll(face, cells_z - 1, 1)

                        mid = state[other, r, i, inner, :]
                        below = state[other, r, i - 1, inner, :] if i > 0 else halo(0)
                        above = state[other, r, i + 1, inner, :] if i < pairs - 1 else halo(1)
                        field = w[0] * mid + w[1] * jnp.where(mask, below, above)
                        field = field + w[2] * state[other, r, i, pl.ds(PAD + y0 + 1, ROWS), :]
                        field = field + w[3] * state[other, r, i, pl.ds(PAD + y0 - 1, ROWS), :]
                        field = field + w[4] * pltpu.roll(mid, cells_z - 1, 1) + w[5] * pltpu.roll(mid, 1, 1)
                        s = state[colour, r, i, inner, :]
                        u_lo = metro[sweep, r, 2 * i, rows, :].astype(jnp.float32)
                        u_hi = metro[sweep, r, 2 * i + 1, rows, :].astype(jnp.float32)
                        u = jnp.where(mask, u_lo, u_hi)
                        accept = jnp.exp2(jnp.minimum(s * field * gain, 0.0))
                        new = s * jnp.tanh((u - accept) * (0.5 / soft_width))
                        rounded = new.astype(jnp.bfloat16)
                        s = rounded.astype(jnp.float32)
                        if last:
                            total = total + s * field
                            a = jnp.where(even, mid, s)
                            b = jnp.where(even, s, mid)
                            swept[r, 2 * i, rows, :] = a.astype(jnp.bfloat16)
                            swept[r, 2 * i + 1, rows, :] = b.astype(jnp.bfloat16)
                        else:
                            state[colour, r, i, inner, :] = s
                if last:
                    esum[lax.rem(r, 2), pl.ds(r // 2, 1), :] = jnp.sum(total, axis=0, keepdims=True)
                else:
                    pack_faces(t + 1, g, rr, r)
                return c

            lax.fori_loop(0, group, one, 0)
            if last:
                swept_to(g).start()
            else:
                for copy in copies(t + 1, g):
                    copy.start()
            for copy in copies(t, g):
                copy.wait_send()
            return carry

        lax.fori_loop(0, groups, one_group, 0)

    def share(value, slots, n, mine, sem0, device):
        erow[sem0] = value
        slots[mine] = value
        sends = []
        for k in range(1, n):
            copy = pltpu.make_async_remote_copy(
                src_ref=erow.at[sem0], dst_ref=slots.at[mine],
                send_sem=esend.at[sem0, k], recv_sem=erecv.at[sem0, k],
                device_id=device(lax.rem(mine + k, n)), device_id_type=MESH)
            copy.start()
            sends.append(copy)
        for copy in sends:
            copy.wait()
        total = slots[0]
        for k in range(1, n):
            total = total + slots[k]
        return total

    mine = jnp.sum(esum[...], axis=2, keepdims=True) + jnp.zeros(erow.shape[1:], jnp.float32)
    total = share(mine, eslot_y, ny, gy, 0, lambda d: (gx, d))
    total = share(total, eslot_x, nx, gx, 1, lambda d: (d, gy))
    energies = total * (-1.0 / (cells_x * nx * cells_y * ny * cells_z))
    row = lax.broadcasted_iota(jnp.int32, erow.shape[2:], 0)
    gap = jnp.zeros(erow.shape[2:], jnp.float32)
    draw = jnp.ones(erow.shape[2:], jnp.float32)
    for k in range(replicas // 2):
        gap = jnp.where(row == k, betas[2 * k] - betas[2 * k + 1], gap)
        draw = jnp.where(row == k, swaps[k], draw)
    delta = swap_gain * gap * (energies[0] - energies[1])
    mix = jax.nn.sigmoid((jnp.minimum(delta, 0.0) - jnp.log(draw)) / swap_width)
    lane = lax.broadcasted_iota(jnp.int32, erow.shape[2:], 1)
    spread = jnp.where(lane == 2 * row, energies[0], 0.0) + jnp.where(lane == 2 * row + 1, energies[1], 0.0)
    info_out[0:1, :] = jnp.sum(spread, axis=0, keepdims=True)
    info_out[1:2, :] = jnp.sum(jnp.where(lane == row, mix, 0.0), axis=0, keepdims=True)
    for g in range(groups):
        swept_to(g).wait()


def exchange(per, info, swept, out, energy_out):
    step = pl.program_id(0)

    @pl.when(step == 0)
    def _():
        for r in range(energy_out.shape[0]):
            energy_out[r] = info[0, r]

    for k in range(per):
        weight = info[1, step * per + k]
        upper = swept[2 * k].astype(jnp.float32)
        lower = swept[2 * k + 1].astype(jnp.float32)
        out[2 * k] = ((1.0 - weight) * upper + weight * lower).astype(jnp.bfloat16)
        out[2 * k + 1] = ((1.0 - weight) * lower + weight * upper).astype(jnp.bfloat16)


def solution(mesh):
    nx, ny = mesh.shape["gx"], mesh.shape["gy"]

    def body(spins, couplings, betas, metro_uniform, swap_uniform):
        replicas, cells_x, cells_y, cells_z = spins.shape
        sweeps = metro_uniform.shape[0]
        pairs, steps, duos = cells_x // 2, 2 * sweeps, replicas // 2
        group = 4 // pairs
        groups = replicas // group
        f32, bf16 = jnp.float32, jnp.bfloat16
        vmem = pl.BlockSpec(memory_space=pltpu.VMEM)
        hbm = pl.BlockSpec(memory_space=pl.ANY)
        smem = pl.BlockSpec(memory_space=pltpu.SMEM)
        lanes = 128
        xface = (steps, groups, 2, group, cells_y // 2, cells_z)
        yface = (steps, groups, 2, group * pairs, cells_z)
        swept, info = pl.pallas_call(
            functools.partial(kernel, nx, ny, group),
            out_shape=(
                jax.ShapeDtypeStruct(spins.shape, bf16),
                jax.ShapeDtypeStruct((2, lanes), f32),
            ),
            in_specs=[hbm, hbm, hbm, smem, smem],
            out_specs=(hbm, vmem),
            scratch_shapes=[
                pltpu.VMEM(spins.shape, bf16),
                pltpu.VMEM(couplings.shape, jnp.int32),
                pltpu.VMEM(metro_uniform.shape, bf16),
                pltpu.VMEM(spins.shape, bf16),
                pltpu.SemaphoreType.DMA((groups,)),
                pltpu.SemaphoreType.DMA,
                pltpu.SemaphoreType.DMA((sweeps, groups)),
                pltpu.SemaphoreType.DMA((groups,)),
                pltpu.VMEM((2, replicas, pairs, cells_y + 2 * PAD, cells_z), f32),
                pltpu.VMEM((2, 6, pairs, cells_y, cells_z), f32),
                pltpu.VMEM(xface, bf16),
                pltpu.VMEM(xface, bf16),
                pltpu.VMEM(yface, f32),
                pltpu.VMEM(yface, f32),
                pltpu.VMEM((2, duos, cells_z), f32),
                pltpu.VMEM((2, 2, duos, lanes), f32),
                pltpu.VMEM((ny, 2, duos, lanes), f32),
                pltpu.VMEM((nx, 2, duos, lanes), f32),
                pltpu.SemaphoreType.DMA((steps, groups, 4)),
                pltpu.SemaphoreType.DMA((steps, groups, 4)),
                pltpu.SemaphoreType.DMA((2, max(nx, ny))),
                pltpu.SemaphoreType.DMA((2, max(nx, ny))),
            ],
            compiler_params=pltpu.CompilerParams(
                collective_id=0, has_side_effects=True, vmem_limit_bytes=60 * 1024 * 1024
            ),
        )(spins, couplings, metro_uniform, betas, swap_uniform)
        per = 4
        block = pl.BlockSpec((2 * per,) + spins.shape[1:], lambda k: (k, 0, 0, 0))
        return pl.pallas_call(
            functools.partial(exchange, per),
            grid=(duos // per,),
            out_shape=(
                jax.ShapeDtypeStruct(spins.shape, bf16),
                jax.ShapeDtypeStruct((replicas,), f32),
            ),
            in_specs=[smem, block],
            out_specs=(block, smem),
        )(info, swept)

    in_specs = (
        P(None, "gx", "gy", None),
        P(None, "gx", "gy", None),
        P(),
        P(None, None, "gx", "gy", None),
        P(),
    )
    out_specs = (P(None, "gx", "gy", None), P())
    return jax.shard_map(body, mesh=mesh, in_specs=in_specs, out_specs=out_specs, check_vma=False)
```

```python
import functools

import jax
import jax.numpy as jnp
from jax import lax
from jax.experimental import pallas as pl
from jax.experimental.pallas import tpu as pltpu
from jax.sharding import PartitionSpec as P

MESH = pl.DeviceIdType.MESH
LOG2E = 1.4426950408889634
PAD = 8
ROWS = 16

soft_width = 0.1
swap_width = 0.25
swap_gain = 64.0


def kernel(
    nx, ny, group,
    spins_hbm, bonds_hbm, metro_hbm, betas, swaps,
    swept_hbm, info_out,
    spins, bonds, metro, swept, spins_sem, bonds_sem, metro_sem, swept_sem,
    state, weights, xsend, xrecv, ysend, yrecv, esum, erow, eslot_y, eslot_x,
    ssem, rsem, esend, erecv,
):
    replicas, cells_x, cells_y, cells_z = spins.shape
    sweeps = metro.shape[0]
    pairs = cells_x // 2
    half = cells_y // 2
    groups = replicas // group
    chunks = cells_y // ROWS
    steps = 2 * sweeps
    gx = lax.axis_index("gx")
    gy = lax.axis_index("gy")
    up_x, down_x = lax.rem(gx + 1, nx), lax.rem(gx + nx - 1, nx)
    up_y, down_y = lax.rem(gy + 1, ny), lax.rem(gy + ny - 1, ny)

    def part(g):
        return pl.ds(g * group, group)

    def spins_in(g):
        return pltpu.make_async_copy(spins_hbm.at[part(g)], spins.at[part(g)], spins_sem.at[g])

    def metro_in(sweep, g):
        return pltpu.make_async_copy(
            metro_hbm.at[sweep, part(g)], metro.at[sweep, part(g)], metro_sem.at[sweep, g])

    def swept_to(g):
        return pltpu.make_async_copy(swept.at[part(g)], swept_hbm.at[part(g)], swept_sem.at[g])

    bonds_in = pltpu.make_async_copy(bonds_hbm, bonds, bonds_sem)
    for g in range(groups):
        spins_in(g).start()

    barrier = pltpu.get_barrier_semaphore()
    for k in range(1, nx):
        pl.semaphore_signal(barrier, inc=1, device_id=(lax.rem(gx + k, nx), gy), device_id_type=MESH)
    for k in range(1, ny):
        pl.semaphore_signal(barrier, inc=1, device_id=(gx, lax.rem(gy + k, ny)), device_id_type=MESH)

    yz = lax.broadcasted_iota(jnp.int32, (ROWS, cells_z), 0) + lax.broadcasted_iota(jnp.int32, (ROWS, cells_z), 1)
    even = (yz & 1) == 0

    def low(colour):
        return even if colour == 0 else jnp.logical_not(even)

    def copies(t, g):
        out = []
        for side, target in enumerate(((up_x, gy), (down_x, gy))):
            out.append(pltpu.make_async_remote_copy(
                src_ref=xsend.at[t, g, side], dst_ref=xrecv.at[t, g, side],
                send_sem=ssem.at[t, g, side], recv_sem=rsem.at[t, g, side],
                device_id=target, device_id_type=MESH))
        for side, target in enumerate(((gx, up_y), (gx, down_y))):
            out.append(pltpu.make_async_remote_copy(
                src_ref=ysend.at[t, g, side], dst_ref=yrecv.at[t, g, side],
                send_sem=ssem.at[t, g, 2 + side], recv_sem=rsem.at[t, g, 2 + side],
                device_id=target, device_id_type=MESH))
        return out

    def pack_faces(t, g, rr, r):
        colour = t % 2
        mask = low(colour)
        other = 1 - colour
        for y0 in range(0, half, ROWS):
            for side, plane in ((0, pairs - 1), (1, 0)):
                near = state[other, r, plane, pl.ds(PAD + y0, ROWS), :]
                far = pltpu.roll(state[other, r, plane, pl.ds(PAD + half + y0, ROWS), :], 1, 1)
                face = jnp.where(mask, near, far) if side == 0 else jnp.where(mask, far, near)
                xsend[t, g, side, rr, pl.ds(y0, ROWS), :] = face.astype(jnp.bfloat16)
        for i in range(pairs):
            ysend[t, g, 0, pl.ds(rr * pairs + i, 1), :] = state[other, r, i, pl.ds(PAD + cells_y - 1, 1), :]
            ysend[t, g, 1, pl.ds(rr * pairs + i, 1), :] = state[other, r, i, pl.ds(PAD, 1), :]

    def prepare(g):
        spins_in(g).wait()

        def one(rr, c):
            r = g * group + rr
            for i in range(pairs):
                for n in range(chunks):
                    rows = pl.ds(n * ROWS, ROWS)
                    a = spins[r, 2 * i, rows, :].astype(jnp.float32)
                    b = spins[r, 2 * i + 1, rows, :].astype(jnp.float32)
                    state[0, r, i, pl.ds(PAD + n * ROWS, ROWS), :] = jnp.where(even, a, b)
                    state[1, r, i, pl.ds(PAD + n * ROWS, ROWS), :] = jnp.where(even, b, a)
            pack_faces(0, g, rr, r)
            return c
        lax.fori_loop(0, group, one, 0)

    def first_group(g, carry):
        prepare(g)
        for copy in copies(0, g):
            copy.start()
        return carry

    prepare(0)
    pl.semaphore_wait(barrier, nx + ny - 2)
    for copy in copies(0, 0):
        copy.start()
    bonds_in.start()
    for sweep in range(sweeps):
        for g in range(groups):
            metro_in(sweep, g).start()
    lax.fori_loop(1, groups, first_group, 0)
    bonds_in.wait()

    def weigh(n, carry):
        rows = pl.ds(pl.multiple_of(n * ROWS, ROWS), ROWS)
        for colour in (0, 1):
            mask = low(colour)
            for i in range(pairs):
                lo, hi = 2 * i, 2 * i + 1
                table = ((0, 3), (3, 0), (1, 1), (4, 4), (2, 2), (5, 5))
                for k, (p, q) in enumerate(table):
                    value = jnp.where(mask, bonds[p, lo, rows, :], bonds[q, hi, rows, :])
                    weights[colour, k, i, rows, :] = value.astype(jnp.float32)
        return carry

    lax.fori_loop(0, chunks, weigh, 0)

    for t in range(steps):
        colour, sweep, other = t % 2, t // 2, 1 - t % 2
        mask = low(colour)
        last = t == steps - 1

        def one_group(g, carry, t=t, colour=colour, sweep=sweep, other=other, mask=mask, last=last):
            if colour == 0:
                metro_in(sweep, g).wait()
            for copy in copies(t, g):
                copy.wait_recv()

            def one(rr, c):
                r = g * group + rr
                gain = betas[r] * (-2.0 * LOG2E)
                for i in range(pairs):
                    row = pl.ds(rr * pairs + i, 1)
                    state[other, r, i, pl.ds(PAD - 1, 1), :] = yrecv[t, g, 0, row, :]
                    state[other, r, i, pl.ds(PAD + cells_y, 1), :] = yrecv[t, g, 1, row, :]
                total = jnp.zeros((ROWS, cells_z), jnp.float32)
                for i in range(pairs):
                    for n in range(chunks):
                        y0 = n * ROWS
                        rows = pl.ds(y0, ROWS)
                        inner = pl.ds(PAD + y0, ROWS)
                        w = [weights[colour, k, i, rows, :] for k in range(6)]

                        def halo(side):
                            face = xrecv[t, g, side, rr, pl.ds(y0 % half, ROWS), :].astype(jnp.float32)
                            return face if y0 < half else pltpu.roll(face, cells_z - 1, 1)

                        mid = state[other, r, i, inner, :]
                        below = state[other, r, i - 1, inner, :] if i > 0 else halo(0)
                        above = state[other, r, i + 1, inner, :] if i < pairs - 1 else halo(1)
                        field = w[0] * mid + w[1] * jnp.where(mask, below, above)
                        field = field + w[2] * state[other, r, i, pl.ds(PAD + y0 + 1, ROWS), :]
                        field = field + w[3] * state[other, r, i, pl.ds(PAD + y0 - 1, ROWS), :]
                        field = field + w[4] * pltpu.roll(mid, cells_z - 1, 1) + w[5] * pltpu.roll(mid, 1, 1)
                        s = state[colour, r, i, inner, :]
                        u_lo = metro[sweep, r, 2 * i, rows, :].astype(jnp.float32)
                        u_hi = metro[sweep, r, 2 * i + 1, rows, :].astype(jnp.float32)
                        u = jnp.where(mask, u_lo, u_hi)
                        accept = jnp.exp2(jnp.minimum(s * field * gain, 0.0))
                        new = s * jnp.tanh((u - accept) * (0.5 / soft_width))
                        rounded = new.astype(jnp.bfloat16)
                        s = rounded.astype(jnp.float32)
                        if last:
                            total = total + s * field
                            a = jnp.where(even, mid, s)
                            b = jnp.where(even, s, mid)
                            swept[r, 2 * i, rows, :] = a.astype(jnp.bfloat16)
                            swept[r, 2 * i + 1, rows, :] = b.astype(jnp.bfloat16)
                        else:
                            state[colour, r, i, inner, :] = s
                if last:
                    esum[lax.rem(r, 2), pl.ds(r // 2, 1), :] = jnp.sum(total, axis=0, keepdims=True)
                else:
                    pack_faces(t + 1, g, rr, r)
                return c

            lax.fori_loop(0, group, one, 0)
            if last:
                swept_to(g).start()
            else:
                for copy in copies(t + 1, g):
                    copy.start()
            for copy in copies(t, g):
                copy.wait_send()
            return carry

        lax.fori_loop(0, groups, one_group, 0)

    def share(value, slots, n, mine, sem0, device):
        erow[sem0] = value
        slots[mine] = value
        sends = []
        for k in range(1, n):
            copy = pltpu.make_async_remote_copy(
                src_ref=erow.at[sem0], dst_ref=slots.at[mine],
                send_sem=esend.at[sem0, k], recv_sem=erecv.at[sem0, k],
                device_id=device(lax.rem(mine + k, n)), device_id_type=MESH)
            copy.start()
            sends.append(copy)
        for copy in sends:
            copy.wait()
        total = slots[0]
        for k in range(1, n):
            total = total + slots[k]
        return total

    mine = jnp.sum(esum[...], axis=2, keepdims=True) + jnp.zeros(erow.shape[1:], jnp.float32)
    total = share(mine, eslot_y, ny, gy, 0, lambda d: (gx, d))
    total = share(total, eslot_x, nx, gx, 1, lambda d: (d, gy))
    energies = total * (-1.0 / (cells_x * nx * cells_y * ny * cells_z))
    row = lax.broadcasted_iota(jnp.int32, erow.shape[2:], 0)
    gap = jnp.zeros(erow.shape[2:], jnp.float32)
    draw = jnp.ones(erow.shape[2:], jnp.float32)
    for k in range(replicas // 2):
        gap = jnp.where(row == k, betas[2 * k] - betas[2 * k + 1], gap)
        draw = jnp.where(row == k, swaps[k], draw)
    delta = swap_gain * gap * (energies[0] - energies[1])
    mix = jax.nn.sigmoid((jnp.minimum(delta, 0.0) - jnp.log(draw)) / swap_width)
    lane = lax.broadcasted_iota(jnp.int32, erow.shape[2:], 1)
    spread = jnp.where(lane == 2 * row, energies[0], 0.0) + jnp.where(lane == 2 * row + 1, energies[1], 0.0)
    info_out[0:1, :] = jnp.sum(spread, axis=0, keepdims=True)
    info_out[1:2, :] = jnp.sum(jnp.where(lane == row, mix, 0.0), axis=0, keepdims=True)
    for g in range(groups):
        swept_to(g).wait()


def exchange(per, info, swept, out, energy_out):
    step = pl.program_id(0)

    @pl.when(step == 0)
    def _():
        for r in range(energy_out.shape[0]):
            energy_out[r] = info[0, r]

    for k in range(per):
        weight = info[1, step * per + k]
        upper = swept[2 * k].astype(jnp.float32)
        lower = swept[2 * k + 1].astype(jnp.float32)
        out[2 * k] = ((1.0 - weight) * upper + weight * lower).astype(jnp.bfloat16)
        out[2 * k + 1] = ((1.0 - weight) * lower + weight * upper).astype(jnp.bfloat16)


def solution(mesh):
    nx, ny = mesh.shape["gx"], mesh.shape["gy"]

    def body(spins, couplings, betas, metro_uniform, swap_uniform):
        replicas, cells_x, cells_y, cells_z = spins.shape
        sweeps = metro_uniform.shape[0]
        pairs, steps, duos = cells_x // 2, 2 * sweeps, replicas // 2
        group = 4 // pairs
        groups = replicas // group
        f32, bf16 = jnp.float32, jnp.bfloat16
        vmem = pl.BlockSpec(memory_space=pltpu.VMEM)
        hbm = pl.BlockSpec(memory_space=pl.ANY)
        smem = pl.BlockSpec(memory_space=pltpu.SMEM)
        lanes = 128
        xface = (steps, groups, 2, group, cells_y // 2, cells_z)
        yface = (steps, groups, 2, group * pairs, cells_z)
        swept, info = pl.pallas_call(
            functools.partial(kernel, nx, ny, group),
            out_shape=(
                jax.ShapeDtypeStruct(spins.shape, bf16),
                jax.ShapeDtypeStruct((2, lanes), f32),
            ),
            in_specs=[hbm, hbm, hbm, smem, smem],
            out_specs=(hbm, vmem),
            scratch_shapes=[
                pltpu.VMEM(spins.shape, bf16),
                pltpu.VMEM(couplings.shape, jnp.int32),
                pltpu.VMEM(metro_uniform.shape, bf16),
                pltpu.VMEM(spins.shape, bf16),
                pltpu.SemaphoreType.DMA((groups,)),
                pltpu.SemaphoreType.DMA,
                pltpu.SemaphoreType.DMA((sweeps, groups)),
                pltpu.SemaphoreType.DMA((groups,)),
                pltpu.VMEM((2, replicas, pairs, cells_y + 2 * PAD, cells_z), f32),
                pltpu.VMEM((2, 6, pairs, cells_y, cells_z), f32),
                pltpu.VMEM(xface, bf16),
                pltpu.VMEM(xface, bf16),
                pltpu.VMEM(yface, f32),
                pltpu.VMEM(yface, f32),
                pltpu.VMEM((2, duos, cells_z), f32),
                pltpu.VMEM((2, 2, duos, lanes), f32),
                pltpu.VMEM((ny, 2, duos, lanes), f32),
                pltpu.VMEM((nx, 2, duos, lanes), f32),
                pltpu.SemaphoreType.DMA((steps, groups, 4)),
                pltpu.SemaphoreType.DMA((steps, groups, 4)),
                pltpu.SemaphoreType.DMA((2, max(nx, ny))),
                pltpu.SemaphoreType.DMA((2, max(nx, ny))),
            ],
            compiler_params=pltpu.CompilerParams(
                collective_id=0, has_side_effects=True, vmem_limit_bytes=60 * 1024 * 1024
            ),
        )(spins, couplings, metro_uniform, betas, swap_uniform)
        per = 4
        block = pl.BlockSpec((2 * per,) + spins.shape[1:], lambda k: (k, 0, 0, 0))
        return pl.pallas_call(
            functools.partial(exchange, per),
            grid=(duos // per,),
            out_shape=(
                jax.ShapeDtypeStruct(spins.shape, bf16),
                jax.ShapeDtypeStruct((replicas,), f32),
            ),
            in_specs=[smem, block],
            out_specs=(block, smem),
        )(info, swept)

    in_specs = (
        P(None, "gx", "gy", None),
        P(None, "gx", "gy", None),
        P(),
        P(None, None, "gx", "gy", None),
        P(),
    )
    out_specs = (P(None, "gx", "gy", None), P())
    return jax.shard_map(body, mesh=mesh, in_specs=in_specs, out_specs=out_specs, check_vma=False)
```

```python
import functools

import jax
import jax.numpy as jnp
from jax import lax
from jax.experimental import pallas as pl
from jax.experimental.pallas import tpu as pltpu
from jax.sharding import PartitionSpec as P

MESH = pl.DeviceIdType.MESH
LOG2E = 1.4426950408889634
PAD = 8
ROWS = 16

soft_width = 0.1
swap_width = 0.25
swap_gain = 64.0


def kernel(
    nx, ny, group,
    spins_hbm, bonds_hbm, metro_hbm, betas, swaps,
    swept_hbm, info_out,
    spins, bonds, metro, swept, spins_sem, bonds_sem, metro_sem, swept_sem,
    state, weights, xsend, xrecv, ysend, yrecv, esum, erow, eslot_y, eslot_x,
    ssem, rsem, esend, erecv,
):
    replicas, cells_x, cells_y, cells_z = spins.shape
    sweeps = metro.shape[0]
    pairs = cells_x // 2
    half = cells_y // 2
    groups = replicas // group
    chunks = cells_y // ROWS
    steps = 2 * sweeps
    gx = lax.axis_index("gx")
    gy = lax.axis_index("gy")
    up_x, down_x = lax.rem(gx + 1, nx), lax.rem(gx + nx - 1, nx)
    up_y, down_y = lax.rem(gy + 1, ny), lax.rem(gy + ny - 1, ny)

    def part(g):
        return pl.ds(g * group, group)

    def spins_in(g):
        return pltpu.make_async_copy(spins_hbm.at[part(g)], spins.at[part(g)], spins_sem.at[g])

    def metro_in(sweep, g):
        return pltpu.make_async_copy(
            metro_hbm.at[sweep, part(g)], metro.at[sweep, part(g)], metro_sem.at[sweep, g])

    def swept_to(g):
        return pltpu.make_async_copy(swept.at[part(g)], swept_hbm.at[part(g)], swept_sem.at[g])

    bonds_in = pltpu.make_async_copy(bonds_hbm, bonds, bonds_sem)
    for g in range(groups):
        spins_in(g).start()

    barrier = pltpu.get_barrier_semaphore()
    for k in range(1, nx):
        pl.semaphore_signal(barrier, inc=1, device_id=(lax.rem(gx + k, nx), gy), device_id_type=MESH)
    for k in range(1, ny):
        pl.semaphore_signal(barrier, inc=1, device_id=(gx, lax.rem(gy + k, ny)), device_id_type=MESH)

    bonds_in.start()
    for sweep in range(sweeps):
        for g in range(groups):
            metro_in(sweep, g).start()

    yz = lax.broadcasted_iota(jnp.int32, (ROWS, cells_z), 0) + lax.broadcasted_iota(jnp.int32, (ROWS, cells_z), 1)
    even = (yz & 1) == 0

    def low(colour):
        return even if colour == 0 else jnp.logical_not(even)

    def copies(t, g):
        out = []
        for side, target in enumerate(((gx, up_y), (gx, down_y))):
            out.append(pltpu.make_async_remote_copy(
                src_ref=ysend.at[t, g, side], dst_ref=yrecv.at[t, g, side],
                send_sem=ssem.at[t, g, 2 + side], recv_sem=rsem.at[t, g, 2 + side],
                device_id=target, device_id_type=MESH))
        for side, target in enumerate(((up_x, gy), (down_x, gy))):
            out.append(pltpu.make_async_remote_copy(
                src_ref=xsend.at[t, g, side], dst_ref=xrecv.at[t, g, side],
                send_sem=ssem.at[t, g, side], recv_sem=rsem.at[t, g, side],
                device_id=target, device_id_type=MESH))
        return out

    def pack_faces(t, g, rr, r):
        colour = t % 2
        mask = low(colour)
        other = 1 - colour
        for y0 in range(0, half, ROWS):
            for side, plane in ((0, pairs - 1), (1, 0)):
                near = state[other, r, plane, pl.ds(PAD + y0, ROWS), :]
                far = pltpu.roll(state[other, r, plane, pl.ds(PAD + half + y0, ROWS), :], 1, 1)
                face = jnp.where(mask, near, far) if side == 0 else jnp.where(mask, far, near)
                xsend[t, g, side, rr, pl.ds(y0, ROWS), :] = face.astype(jnp.bfloat16)
        for i in range(pairs):
            ysend[t, g, 0, pl.ds(rr * pairs + i, 1), :] = state[other, r, i, pl.ds(PAD + cells_y - 1, 1), :]
            ysend[t, g, 1, pl.ds(rr * pairs + i, 1), :] = state[other, r, i, pl.ds(PAD, 1), :]

    def prepare(g):
        spins_in(g).wait()

        def one(rr, c):
            r = g * group + rr
            for i in range(pairs):
                for n in range(chunks):
                    rows = pl.ds(n * ROWS, ROWS)
                    a = spins[r, 2 * i, rows, :].astype(jnp.float32)
                    b = spins[r, 2 * i + 1, rows, :].astype(jnp.float32)
                    state[0, r, i, pl.ds(PAD + n * ROWS, ROWS), :] = jnp.where(even, a, b)
                    state[1, r, i, pl.ds(PAD + n * ROWS, ROWS), :] = jnp.where(even, b, a)
            pack_faces(0, g, rr, r)
            return c
        lax.fori_loop(0, group, one, 0)

    def first_group(g, carry):
        prepare(g)
        for copy in copies(0, g):
            copy.start()
        return carry

    prepare(0)
    pl.semaphore_wait(barrier, nx + ny - 2)
    for copy in copies(0, 0):
        copy.start()
    lax.fori_loop(1, groups, first_group, 0)
    bonds_in.wait()

    def weigh(n, carry):
        rows = pl.ds(pl.multiple_of(n * ROWS, ROWS), ROWS)
        for colour in (0, 1):
            mask = low(colour)
            for i in range(pairs):
                lo, hi = 2 * i, 2 * i + 1
                table = ((0, 3), (3, 0), (1, 1), (4, 4), (2, 2), (5, 5))
                for k, (p, q) in enumerate(table):
                    value = jnp.where(mask, bonds[p, lo, rows, :], bonds[q, hi, rows, :])
                    weights[colour, k, i, rows, :] = value.astype(jnp.float32)
        return carry

    lax.fori_loop(0, chunks, weigh, 0)

    for t in range(steps):
        colour, sweep, other = t % 2, t // 2, 1 - t % 2
        mask = low(colour)
        last = t == steps - 1

        def one_group(g, carry, t=t, colour=colour, sweep=sweep, other=other, mask=mask, last=last):
            if colour == 0:
                metro_in(sweep, g).wait()
            for copy in copies(t, g):
                copy.wait_recv()

            def one(rr, c):
                r = g * group + rr
                gain = betas[r] * (-2.0 * LOG2E)
                for i in range(pairs):
                    row = pl.ds(rr * pairs + i, 1)
                    state[other, r, i, pl.ds(PAD - 1, 1), :] = yrecv[t, g, 0, row, :]
                    state[other, r, i, pl.ds(PAD + cells_y, 1), :] = yrecv[t, g, 1, row, :]
                total = jnp.zeros((ROWS, cells_z), jnp.float32)
                for i in range(pairs):
                    for n in range(chunks):
                        y0 = n * ROWS
                        rows = pl.ds(y0, ROWS)
                        inner = pl.ds(PAD + y0, ROWS)
                        w = [weights[colour, k, i, rows, :] for k in range(6)]

                        def halo(side):
                            face = xrecv[t, g, side, rr, pl.ds(y0 % half, ROWS), :].astype(jnp.float32)
                            return face if y0 < half else pltpu.roll(face, cells_z - 1, 1)

                        mid = state[other, r, i, inner, :]
                        below = state[other, r, i - 1, inner, :] if i > 0 else halo(0)
                        above = state[other, r, i + 1, inner, :] if i < pairs - 1 else halo(1)
                        field = w[0] * mid + w[1] * jnp.where(mask, below, above)
                        field = field + w[2] * state[other, r, i, pl.ds(PAD + y0 + 1, ROWS), :]
                        field = field + w[3] * state[other, r, i, pl.ds(PAD + y0 - 1, ROWS), :]
                        field = field + w[4] * pltpu.roll(mid, cells_z - 1, 1) + w[5] * pltpu.roll(mid, 1, 1)
                        s = state[colour, r, i, inner, :]
                        u_lo = metro[sweep, r, 2 * i, rows, :].astype(jnp.float32)
                        u_hi = metro[sweep, r, 2 * i + 1, rows, :].astype(jnp.float32)
                        u = jnp.where(mask, u_lo, u_hi)
                        accept = jnp.exp2(jnp.minimum(s * field * gain, 0.0))
                        new = s * jnp.tanh((u - accept) * (0.5 / soft_width))
                        rounded = new.astype(jnp.bfloat16)
                        s = rounded.astype(jnp.float32)
                        if last:
                            total = total + s * field
                            a = jnp.where(even, mid, s)
                            b = jnp.where(even, s, mid)
                            swept[r, 2 * i, rows, :] = a.astype(jnp.bfloat16)
                            swept[r, 2 * i + 1, rows, :] = b.astype(jnp.bfloat16)
                        else:
                            state[colour, r, i, inner, :] = s
                if last:
                    esum[lax.rem(r, 2), pl.ds(r // 2, 1), :] = jnp.sum(total, axis=0, keepdims=True)
                else:
                    pack_faces(t + 1, g, rr, r)
                return c

            lax.fori_loop(0, group, one, 0)
            if last:
                swept_to(g).start()
            else:
                for copy in copies(t + 1, g):
                    copy.start()
            for copy in copies(t, g):
                copy.wait_send()
            return carry

        lax.fori_loop(0, groups, one_group, 0)

    def share(value, slots, n, mine, sem0, device):
        erow[sem0] = value
        slots[mine] = value
        sends = []
        for k in range(1, n):
            copy = pltpu.make_async_remote_copy(
                src_ref=erow.at[sem0], dst_ref=slots.at[mine],
                send_sem=esend.at[sem0, k], recv_sem=erecv.at[sem0, k],
                device_id=device(lax.rem(mine + k, n)), device_id_type=MESH)
            copy.start()
            sends.append(copy)
        for copy in sends:
            copy.wait()
        total = slots[0]
        for k in range(1, n):
            total = total + slots[k]
        return total

    mine = jnp.sum(esum[...], axis=2, keepdims=True) + jnp.zeros(erow.shape[1:], jnp.float32)
    total = share(mine, eslot_y, ny, gy, 0, lambda d: (gx, d))
    total = share(total, eslot_x, nx, gx, 1, lambda d: (d, gy))
    energies = total * (-1.0 / (cells_x * nx * cells_y * ny * cells_z))
    row = lax.broadcasted_iota(jnp.int32, erow.shape[2:], 0)
    gap = jnp.zeros(erow.shape[2:], jnp.float32)
    draw = jnp.ones(erow.shape[2:], jnp.float32)
    for k in range(replicas // 2):
        gap = jnp.where(row == k, betas[2 * k] - betas[2 * k + 1], gap)
        draw = jnp.where(row == k, swaps[k], draw)
    delta = swap_gain * gap * (energies[0] - energies[1])
    mix = jax.nn.sigmoid((jnp.minimum(delta, 0.0) - jnp.log(draw)) / swap_width)
    lane = lax.broadcasted_iota(jnp.int32, erow.shape[2:], 1)
    spread = jnp.where(lane == 2 * row, energies[0], 0.0) + jnp.where(lane == 2 * row + 1, energies[1], 0.0)
    info_out[0:1, :] = jnp.sum(spread, axis=0, keepdims=True)
    info_out[1:2, :] = jnp.sum(jnp.where(lane == row, mix, 0.0), axis=0, keepdims=True)
    for g in range(groups):
        swept_to(g).wait()


def exchange(per, info, swept, out, energy_out):
    step = pl.program_id(0)

    @pl.when(step == 0)
    def _():
        for r in range(energy_out.shape[0]):
            energy_out[r] = info[0, r]

    for k in range(per):
        weight = info[1, step * per + k]
        upper = swept[2 * k].astype(jnp.float32)
        lower = swept[2 * k + 1].astype(jnp.float32)
        out[2 * k] = ((1.0 - weight) * upper + weight * lower).astype(jnp.bfloat16)
        out[2 * k + 1] = ((1.0 - weight) * lower + weight * upper).astype(jnp.bfloat16)


def solution(mesh):
    nx, ny = mesh.shape["gx"], mesh.shape["gy"]

    def body(spins, couplings, betas, metro_uniform, swap_uniform):
        replicas, cells_x, cells_y, cells_z = spins.shape
        sweeps = metro_uniform.shape[0]
        pairs, steps, duos = cells_x // 2, 2 * sweeps, replicas // 2
        group = 4 // pairs
        groups = replicas // group
        f32, bf16 = jnp.float32, jnp.bfloat16
        vmem = pl.BlockSpec(memory_space=pltpu.VMEM)
        hbm = pl.BlockSpec(memory_space=pl.ANY)
        smem = pl.BlockSpec(memory_space=pltpu.SMEM)
        lanes = 128
        xface = (steps, groups, 2, group, cells_y // 2, cells_z)
        yface = (steps, groups, 2, group * pairs, cells_z)
        swept, info = pl.pallas_call(
            functools.partial(kernel, nx, ny, group),
            out_shape=(
                jax.ShapeDtypeStruct(spins.shape, bf16),
                jax.ShapeDtypeStruct((2, lanes), f32),
            ),
            in_specs=[hbm, hbm, hbm, smem, smem],
            out_specs=(hbm, vmem),
            scratch_shapes=[
                pltpu.VMEM(spins.shape, bf16),
                pltpu.VMEM(couplings.shape, jnp.int32),
                pltpu.VMEM(metro_uniform.shape, bf16),
                pltpu.VMEM(spins.shape, bf16),
                pltpu.SemaphoreType.DMA((groups,)),
                pltpu.SemaphoreType.DMA,
                pltpu.SemaphoreType.DMA((sweeps, groups)),
                pltpu.SemaphoreType.DMA((groups,)),
                pltpu.VMEM((2, replicas, pairs, cells_y + 2 * PAD, cells_z), f32),
                pltpu.VMEM((2, 6, pairs, cells_y, cells_z), f32),
                pltpu.VMEM(xface, bf16),
                pltpu.VMEM(xface, bf16),
                pltpu.VMEM(yface, f32),
                pltpu.VMEM(yface, f32),
                pltpu.VMEM((2, duos, cells_z), f32),
                pltpu.VMEM((2, 2, duos, lanes), f32),
                pltpu.VMEM((ny, 2, duos, lanes), f32),
                pltpu.VMEM((nx, 2, duos, lanes), f32),
                pltpu.SemaphoreType.DMA((steps, groups, 4)),
                pltpu.SemaphoreType.DMA((steps, groups, 4)),
                pltpu.SemaphoreType.DMA((2, max(nx, ny))),
                pltpu.SemaphoreType.DMA((2, max(nx, ny))),
            ],
            compiler_params=pltpu.CompilerParams(
                collective_id=0, has_side_effects=True, vmem_limit_bytes=60 * 1024 * 1024
            ),
        )(spins, couplings, metro_uniform, betas, swap_uniform)
        per = 4
        block = pl.BlockSpec((2 * per,) + spins.shape[1:], lambda k: (k, 0, 0, 0))
        return pl.pallas_call(
            functools.partial(exchange, per),
            grid=(duos // per,),
            out_shape=(
                jax.ShapeDtypeStruct(spins.shape, bf16),
                jax.ShapeDtypeStruct((replicas,), f32),
            ),
            in_specs=[smem, block],
            out_specs=(block, smem),
        )(info, swept)

    in_specs = (
        P(None, "gx", "gy", None),
        P(None, "gx", "gy", None),
        P(),
        P(None, None, "gx", "gy", None),
        P(),
    )
    out_specs = (P(None, "gx", "gy", None), P())
    return jax.shard_map(body, mesh=mesh, in_specs=in_specs, out_specs=out_specs, check_vma=False)
```
